512 devices in a mesh: grp: 8 (over z_hi, core), blk: 64 (over y, x, z_lo).
Axes of the slice: x: 4, y: 8, z: 8 (z_hi: 4, z_lo: 2; z = z_hi * 2 + z_lo), core: 2. Of those that a mesh axis runs over, the one named last changes fastest.
Arguments:
- ints: bfloat16 [64, 1536, 4096], P('blk', 'grp'), may hold values from -1 to 1
- occ_energy: float32 [400], replicated, may hold values from -2 to -0.3
- occ_window: int32 [64], replicated, may hold values from 0 to 399, as said below
- virt_energy: float32 [1536], replicated, may hold values from 0.3 to 3
Outputs:
- virt_density: float32 [1536, 192], P(('grp', 'blk'))
- pair_energy: float32 [64, 4], P('blk')
The draws below stay inside these ranges and needn't reach their ends.
Inputs may be any that keep to these rules, and one draw needn't show every extreme that they name: `occ_window`: distinct indices into occ_energy.
All inputs are finite; a program needn't handle non-finite values.
Results may differ from the reference program's by a relative error of at most 0.0003.
Values may be sent and summed in bfloat16 or wider, within the bound.
No kernel may reach another device: no remote copies, remote signals or barrier semaphores. Data moves between devices by JAX's collectives and lax.ppermute only.
A program may use at most 64 MiB of HBM per device.

```python
import jax
import jax.numpy as jnp
from jax import lax

NVIRT = 1536
NAUX = 4096
NOCC_ALL = 400
OCC_DEV = 1
STEPS = 4
NOCC = 64
N_GRP = 8
N_BLK = 64


def draw_occ_window(key, part):
    return jax.random.permutation(key, NOCC_ALL)[:NOCC].astype(jnp.int32)


def spiked(array, rng, source, target, parts, factor):
    owner, partner = [(jnp.arange(array.shape[axis_at]) // (array.shape[axis_at] // parts)).reshape([-1 if axis == axis_at else 1 for axis in range(array.ndim)]) for axis_at in (source, target)]
    chosen = jax.random.permutation(rng, parts)[partner]
    strong = (owner == chosen) | (owner == (partner + parts // 2) % parts)
    return jnp.where(strong, factor * array, array)


def steps_of(stream_key, dims, split, least, largest):
    gain, own = 1.0, jax.random.fold_in(stream_key, 6)
    for position, shards_of in split:
        steps = jnp.exp(jax.random.uniform(jax.random.fold_in(own, position), (shards_of,), jnp.float32, least / len(split), largest / len(split)))
        gain = gain * jnp.repeat(steps, dims[position] // shards_of).reshape([-1 if axis == position else 1 for axis in range(len(dims))])
    return gain


def bell_draw_with(stream_key, dims, scale, reach, shards, heavy, kind=jnp.bfloat16):
    drawn = scale * jax.random.normal(stream_key, dims, jnp.float32)
    if shards:
        drawn = drawn * steps_of(stream_key, dims, shards, -0.22, 0.18)
    return jnp.clip(spiked(drawn, jax.random.fold_in(stream_key, 3), *heavy), -reach, reach).astype(kind)


def setup_inputs(seed: int = 0) -> dict:
    keys = jax.random.split(jax.random.key(seed), 5)
    ints = bell_draw_with(keys[0], (NOCC, NVIRT, NAUX), (0.5 * NAUX ** -0.25), 1.0, ((0, 64), (1, 8)), (0, 1, 64, 4.0))
    occ_energy = jnp.clip(jax.random.uniform(keys[1], (NOCC_ALL,), jnp.float32, -2.0, -0.3), -2.0, -0.3)
    occ_window = draw_occ_window(jax.random.fold_in(keys[4], 71), 0)
    virt_energy = jnp.clip(jax.random.uniform(keys[3], (NVIRT,), jnp.float32, 0.3, 3.0), 0.3, 3.0)
    return {"ints": ints, "occ_energy": occ_energy, "occ_window": occ_window, "virt_energy": virt_energy}


def reference(ints, occ_energy, occ_window, virt_energy):
    occ_levels = occ_energy[occ_window]
    block_size = NVIRT // N_GRP
    pair_blocks = N_GRP // 2
    virt_pairs = virt_energy.reshape(pair_blocks, 2 * block_size)
    window_pos = jnp.arange(NOCC, dtype=jnp.int32)
    density = jnp.zeros((NVIRT, block_size), jnp.float32)
    energy_list = []
    for cycle_step in range(STEPS):
        for within in range(OCC_DEV):
            partner_idx = (((window_pos // OCC_DEV - cycle_step) % N_BLK) * OCC_DEV + within).astype(jnp.int32)
            occ_partner = occ_levels[partner_idx]

            def single_pair(inputs_in):
                row_ints, partner_at, occ_row, occ_col = inputs_in
                col_ints = lax.dynamic_index_in_dim(ints, partner_at, 0, keepdims=False)
                left = row_ints.astype(jnp.float32).reshape(pair_blocks, 2 * block_size, NAUX)
                right = col_ints.astype(jnp.float32).reshape(pair_blocks, 2 * block_size, NAUX)
                coupling = jnp.einsum('qap,qbp->qab', left, right, precision=lax.Precision.HIGHEST)
                denominator = virt_pairs[:, :, None] + virt_pairs[:, None, :] - occ_row - occ_col
                amplitude = coupling / denominator
                product = jnp.einsum('qab,qcb->qac', amplitude, amplitude, precision=lax.Precision.HIGHEST)
                blocks = jnp.stack([product[:, :block_size, :block_size], product[:, block_size:, block_size:]], 1)
                pair_value = -jnp.sum(amplitude * coupling) / (block_size * block_size)
                return blocks.reshape(NVIRT, block_size), pair_value

            blocks, values = lax.map(single_pair, (ints, partner_idx, occ_levels, occ_partner))
            density = density + jnp.sum(blocks, axis=0)
            energy_list.append(values)
    return density / (NOCC * STEPS * OCC_DEV), jnp.stack(energy_list, axis=1)
```

```python
import functools

import jax
import jax.numpy as jnp
from jax import lax
from jax.experimental import pallas as pl
from jax.experimental.pallas import tpu as pltpu
from jax.sharding import Mesh
from jax.sharding import PartitionSpec as P

STEPS = 4
CHUNKS = 4
GRP = ("z_hi", "core")
VMEM_BYTES = 24 * 1024 * 1024


def shifted(shard, axis, by):
    peers = lax.axis_size(axis)
    return lax.ppermute(shard, axis, [(i, (i + by) % peers) for i in range(peers)])


def nt_dot(left, right):
    return lax.dot_general(
        left, right, (((1,), (1,)), ((), ())), preferred_element_type=jnp.float32
    )


def self_product(amps):
    head = amps.astype(jnp.bfloat16)
    rest = (amps - head.astype(jnp.float32)).astype(jnp.bfloat16)
    return nt_dot(head, head) + nt_dot(head, rest) + nt_dot(rest, head)


def amplitude_of(coupling, virt_col, virt_row, occ_row, occ_partner):
    return coupling / (virt_col + virt_row - occ_row - occ_partner)


def own_kernel(levels, own, own_mirror, virt_col, virt_rows, density, energy):
    total = jnp.zeros(density.shape, jnp.float32)
    value = jnp.zeros((1, 1), jnp.float32)
    for half, cols in enumerate((own, own_mirror)):
        coupling = nt_dot(own[...], cols[...])
        amp = amplitude_of(
            coupling, virt_col[...], virt_rows[half : half + 1, :], levels[0], levels[0]
        )
        value = value + jnp.sum(amp * coupling, keepdims=True)
        total = total + self_product(amp)
    density[...] = total
    energy[...] = jnp.broadcast_to(value, energy.shape)


def pair_list(own, own_mirror, near, far, far_mirror):
    return (
        (own, far),
        (own, far_mirror),
        (near, own),
        (near, own_mirror),
        (near, far),
        (near, far_mirror),
    )


def chunk_kernel(first, own, own_mirror, near, far, far_mirror, *rest):
    sums = rest[-1]
    for at, (rows, cols) in enumerate(pair_list(own, own_mirror, near, far, far_mirror)):
        part = nt_dot(rows[...], cols[...])
        sums[at] = part if first else rest[0][at] + part


def last_kernel(
    levels,
    own,
    own_mirror,
    near,
    far,
    far_mirror,
    sums,
    virt_col,
    virt_rows,
    density_in,
    energy_in,
    density_out,
    energy_out,
    held,
):
    pairs = pair_list(own, own_mirror, near, far, far_mirror)
    total = density_in[...]
    values = []
    for at, (rows, cols) in enumerate(pairs):
        coupling = sums[at] + nt_dot(rows[...], cols[...])
        left = levels[0] if at < 2 else levels[1]
        right = levels[0] if at in (2, 3) else levels[2]
        amp = amplitude_of(
            coupling, virt_col[...], virt_rows[at % 2 : at % 2 + 1, :], left, right
        )
        values.append(jnp.sum(amp * coupling, keepdims=True))
        total = total + self_product(amp)
    own_two = values[0] + values[1]
    next_one = values[2] + values[3]
    next_three = values[4] + values[5]
    lane = lax.broadcasted_iota(jnp.int32, energy_out.shape, 1)
    picked = jnp.where(lane == 0, energy_in[...], 0.0)
    picked = jnp.where(lane == 1, own_two, picked)
    picked = jnp.where(lane == 2, next_one, picked)
    picked = jnp.where(lane == 3, next_three, picked)
    energy_out[...] = picked
    lanes = held.shape[2]
    panels = held.shape[0]
    width = total.shape[1]
    for panel in range(panels):
        part = total[:, panel * lanes : min(width, (panel + 1) * lanes)]
        if part.shape[1] < lanes:
            held[panel] = jnp.zeros(held.shape[1:], jnp.float32)
        held[panel, :, : part.shape[1]] = part
    peers, span = density_out.shape
    rows_each = width // peers
    for row in range(rows_each):
        for panel in range(panels):
            at = (row * panels + panel) * lanes
            density_out[:, at : at + lanes] = held[panel, pl.Slice(row, peers, rows_each), :]


def lookup_many(values_in, where_at):
    positions = jnp.arange(values_in.shape[0], dtype=jnp.int32)
    matches = positions[None, :] == where_at[:, None]
    return jnp.sum(
        jnp.where(matches, values_in[None, :], jnp.zeros_like(values_in)[None, :]), axis=1
    )


def call(kernel, out_shape, operands, smem=0, scratch=(), flops=0, moved=0):
    vmem = pl.BlockSpec(memory_space=pltpu.VMEM)
    specs = [pl.BlockSpec(memory_space=pltpu.SMEM)] * smem
    specs += [vmem] * (len(operands) - smem)
    outs = jax.tree.map(lambda _: vmem, out_shape)
    return pl.pallas_call(
        kernel,
        out_shape=out_shape,
        in_specs=specs,
        out_specs=outs,
        scratch_shapes=list(scratch),
        compiler_params=pltpu.CompilerParams(vmem_limit_bytes=VMEM_BYTES),
        cost_estimate=pl.CostEstimate(flops=flops, bytes_accessed=moved, transcendentals=0),
    )(*operands)


def local(ints, occ_energy, occ_window, virt_energy):
    own = ints[0]
    width, depth = own.shape
    piece = depth // CHUNKS
    occ_count = occ_window.shape[0]
    peers = lax.axis_size("blk")
    group_index = lax.axis_index(GRP)
    block_index = lax.axis_index("blk")
    mirror_index = group_index + 1 - 2 * (group_index % 2)

    cut = [own[:, c * piece : (c + 1) * piece] for c in range(CHUNKS)]
    far = [shifted(part, "blk", 2) for part in cut]
    near = [shifted(part, "blk", -1) for part in cut]
    own_mirror = shifted(own, "core", 1)
    far_mirror = [shifted(part, "core", 1) for part in far]

    virt_own = lax.dynamic_slice_in_dim(virt_energy, group_index * width, width)
    virt_mirror = lax.dynamic_slice_in_dim(virt_energy, mirror_index * width, width)
    virt_rows = jnp.stack([virt_own, virt_mirror])
    virt_col = virt_own[:, None]
    wanted = (block_index + jnp.array([0, 1, -2], jnp.int32)) % peers
    levels = lookup_many(occ_energy, lookup_many(occ_window, wanted))

    square = jax.ShapeDtypeStruct((width, width), jnp.float32)
    line = jax.ShapeDtypeStruct((1, 128), jnp.float32)
    density, energy = call(
        own_kernel,
        (square, line),
        (levels, own, own_mirror, virt_col, virt_rows),
        smem=1,
        flops=4 * width * width * depth,
        moved=4 * width * depth,
    )
    sums = None
    six = jax.ShapeDtypeStruct((6, width, width), jnp.float32)
    for c in range(CHUNKS):
        blocks = (
            cut[c],
            own_mirror[:, c * piece : (c + 1) * piece],
            near[c],
            far[c],
            far_mirror[c],
        )
        if c < CHUNKS - 1:
            sums = call(
                functools.partial(chunk_kernel, sums is None),
                six,
                blocks + (() if sums is None else (sums,)),
                flops=12 * width * width * piece,
                moved=10 * width * piece,
            )
    rows_each = width // peers
    stride = -(-width // 128) * 128
    spread, energies = call(
        last_kernel,
        (jax.ShapeDtypeStruct((peers, rows_each * stride), jnp.float32), line),
        (levels,) + blocks + (sums, virt_col, virt_rows, density, energy),
        smem=1,
        scratch=(pltpu.VMEM((stride // 128, width, 128), jnp.float32),),
        flops=12 * width * width * piece,
        moved=10 * width * piece,
    )
    arrived = lax.all_to_all(spread, "blk", 0, 0, tiled=True)
    passed = shifted(energies[:, 2:4], "blk", 1)
    pair = jnp.stack([energies[:, 0], passed[:, 0], energies[:, 1], passed[:, 1]], axis=1)
    totals = lax.psum(lax.psum(pair, "core"), "z_hi") * (-1.0 / (width * width))
    share = arrived.sum(axis=0).reshape(rows_each, stride)[:, :width]
    return share * (1.0 / (occ_count * STEPS)), totals


def solution(mesh):
    peers = mesh.shape["blk"]
    finer = Mesh(mesh.devices.reshape(-1, 2, peers), ("z_hi", "core", "blk"))
    placed = (P("blk", GRP, None), P(), P(), P())
    return jax.shard_map(
        local,
        mesh=finer,
        in_specs=placed,
        out_specs=(P(GRP + ("blk",), None), P("blk", None)),
        check_vma=False,
    )
```

```python
import functools

import jax
import jax.numpy as jnp
from jax import lax
from jax.experimental import pallas as pl
from jax.experimental.pallas import tpu as pltpu
from jax.sharding import Mesh
from jax.sharding import PartitionSpec as P

STEPS = 4
LANES = 128
GRP = ("z_hi", "core")
VMEM_BYTES = 8 * 1024 * 1024
OWN_PAIRS = ((0, 0, 0),)
FAR_PAIRS = ((0, 1, 0), (0, 2, 2))
NEAR_PAIRS = ((1, 0, 1), (1, 1, 1), (1, 2, 3))
LAST_PAIRS = ((0, 3, 2), (1, 3, 3))


def shifted(shard, axis, by):
    peers = lax.axis_size(axis)
    return lax.ppermute(shard, axis, [(i, (i + by) % peers) for i in range(peers)])


def nt_dot(left, right):
    return lax.dot_general(
        left, right, (((1,), (1,)), ((), ())), preferred_element_type=jnp.float32
    )


def self_product(amps):
    head = amps.astype(jnp.bfloat16)
    rest = (amps - head.astype(jnp.float32)).astype(jnp.bfloat16)
    return nt_dot(head, head) + nt_dot(head, rest) + nt_dot(rest, head)


def add_pairs(pairs, rows, cols, levels, virt_col, virt_rows, density, energy):
    lane = lax.broadcasted_iota(jnp.int32, energy.shape, 1)
    for row, col, slot in pairs:
        coupling = nt_dot(rows[row][...], cols[col][...])
        half = col % 2
        denominator = (
            virt_col[...]
            + virt_rows[half : half + 1, :]
            - levels[row]
            - levels[0 if col < 2 else 2]
        )
        amp = coupling / denominator
        value = jnp.sum(amp * coupling, keepdims=True)
        energy = energy + jnp.where(lane == slot, value, 0.0)
        density = density + self_product(amp)
    return density, energy


def own_kernel(levels, own, virt_col, virt_rows, density, energy):
    density[...], energy[...] = add_pairs(
        OWN_PAIRS,
        (own,),
        (own,),
        levels,
        virt_col,
        virt_rows,
        jnp.zeros(density.shape, jnp.float32),
        jnp.zeros(energy.shape, jnp.float32),
    )


def far_kernel(
    levels, own, own_mirror, far, virt_col, virt_rows, density_in, energy_in, density, energy
):
    density[...], energy[...] = add_pairs(
        FAR_PAIRS,
        (own,),
        (None, own_mirror, far),
        levels,
        virt_col,
        virt_rows,
        density_in[...],
        energy_in[...],
    )


def near_kernel(
    levels, own, own_mirror, near, far, virt_col, virt_rows, density_in, energy_in, density, energy
):
    density[...], energy[...] = add_pairs(
        NEAR_PAIRS,
        (None, near),
        (own, own_mirror, far),
        levels,
        virt_col,
        virt_rows,
        density_in[...],
        energy_in[...],
    )


def last_kernel(
    levels,
    block,
    own,
    near,
    far_mirror,
    virt_col,
    virt_rows,
    density_in,
    energy_in,
    spread,
    held,
):
    density, energy = add_pairs(
        LAST_PAIRS,
        (own, near),
        (None, None, None, far_mirror),
        levels,
        virt_col,
        virt_rows,
        density_in[...],
        energy_in[...],
    )
    width = density.shape[0]
    peers, rows, stride = spread.shape
    panels = stride // LANES
    for panel in range(panels):
        part = density[:, panel * LANES : min(width, (panel + 1) * LANES)]
        if part.shape[1] < LANES:
            held[panel] = jnp.zeros(held.shape[1:], jnp.float32)
        held[panel, :, : part.shape[1]] = part
    each = width // peers
    for row in range(each):
        for panel in range(panels):
            spread[:, row, panel * LANES : (panel + 1) * LANES] = held[
                panel, pl.Slice(row, peers, each), :
            ]
    owner = lax.broadcasted_iota(jnp.int32, (peers, LANES), 0)
    slot = lax.broadcasted_iota(jnp.int32, (peers, LANES), 1)
    target = jnp.where(slot % 2 == 0, block[0], block[1])
    scaled = energy * (-1.0 / (width * width))
    spread[:, each, :LANES] = jnp.where(owner == target, scaled, 0.0)
    spread[:, each, LANES:] = jnp.zeros((peers, stride - LANES), jnp.float32)


def lookup_many(values_in, where_at):
    positions = jnp.arange(values_in.shape[0], dtype=jnp.int32)
    matches = positions[None, :] == where_at[:, None]
    return jnp.sum(
        jnp.where(matches, values_in[None, :], jnp.zeros_like(values_in)[None, :]), axis=1
    )


def call(kernel, out_shape, operands, smem, pairs, block, scratch=()):
    vmem = pl.BlockSpec(memory_space=pltpu.VMEM)
    specs = [pl.BlockSpec(memory_space=pltpu.SMEM)] * smem
    specs += [vmem] * (len(operands) - smem)
    width, depth = block.shape
    return pl.pallas_call(
        kernel,
        out_shape=out_shape,
        in_specs=specs,
        out_specs=jax.tree.map(lambda _: vmem, out_shape),
        scratch_shapes=list(scratch),
        compiler_params=pltpu.CompilerParams(vmem_limit_bytes=VMEM_BYTES),
        cost_estimate=pl.CostEstimate(
            flops=2 * pairs * width * width * depth,
            bytes_accessed=2 * pairs * width * depth,
            transcendentals=0,
        ),
    )(*operands)


def local(ints, occ_energy, occ_window, virt_energy):
    far = shifted(ints, "blk", 2)[0]
    near = shifted(ints, "blk", -1)[0]
    own_mirror = shifted(ints, "core", 1)[0]
    own = ints[0]
    width, depth = own.shape
    occ_count = occ_window.shape[0]
    peers = lax.axis_size("blk")
    group_index = lax.axis_index(GRP)
    block_index = lax.axis_index("blk")
    mirror_index = group_index + 1 - 2 * (group_index % 2)

    virt_own = lax.dynamic_slice_in_dim(virt_energy, group_index * width, width)
    virt_mirror = lax.dynamic_slice_in_dim(virt_energy, mirror_index * width, width)
    virt = (virt_own[:, None], jnp.stack([virt_own, virt_mirror]))
    wanted = (block_index + jnp.array([0, 1, -2], jnp.int32)) % peers
    levels = lookup_many(occ_energy, lookup_many(occ_window, wanted))

    sums = (
        jax.ShapeDtypeStruct((width, width), jnp.float32),
        jax.ShapeDtypeStruct((1, LANES), jnp.float32),
    )
    state = call(own_kernel, sums, (levels, own) + virt, 1, 1, own)
    far, density, energy = lax.optimization_barrier((far, *state))
    far_mirror = shifted(far, "core", 1)
    state = call(
        far_kernel, sums, (levels, own, own_mirror, far) + virt + (density, energy), 1, 2, own
    )
    state = call(
        near_kernel, sums, (levels, own, own_mirror, near, far) + virt + tuple(state), 1, 3, own
    )
    each = width // peers
    panels = -(-width // LANES)
    spread = call(
        last_kernel,
        jax.ShapeDtypeStruct((peers, each + 1, panels * LANES), jnp.float32),
        (levels, wanted, own, near, far_mirror) + virt + tuple(state),
        2,
        2,
        own,
        scratch=(pltpu.VMEM((panels, width, LANES), jnp.float32),),
    )
    arrived = lax.all_to_all(spread, "blk", 0, 0, tiled=True)
    total = arrived.sum(axis=0)
    pair = lax.psum(lax.psum(total[each:, :STEPS], "core"), "z_hi")
    return total[:each, :width] * (1.0 / (occ_count * STEPS)), pair


def solution(mesh):
    peers = mesh.shape["blk"]
    finer = Mesh(mesh.devices.reshape(-1, 2, peers), ("z_hi", "core", "blk"))
    placed = (P("blk", GRP, None), P(), P(), P())
    return jax.shard_map(
        local,
        mesh=finer,
        in_specs=placed,
        out_specs=(P(GRP + ("blk",), None), P("blk", None)),
        check_vma=False,
    )
```

```python
import functools

import jax
import jax.numpy as jnp
from jax import lax
from jax.experimental import pallas as pl
from jax.experimental.pallas import tpu as pltpu
from jax.sharding import Mesh
from jax.sharding import PartitionSpec as P

STEPS = 4
LANES = 128
GRP = ("z_hi", "core")
VMEM_BYTES = 8 * 1024 * 1024
OWN_PAIRS = ((0, 0, 0),)
FAR_PAIRS = ((0, 1, 0), (0, 2, 2))
NEAR_PAIRS = ((1, 0, 1), (1, 1, 1), (1, 2, 3))
LAST_PAIRS = ((0, 3, 2), (1, 3, 3))


def shifted(shard, axis, by):
    peers = lax.axis_size(axis)
    return lax.ppermute(shard, axis, [(i, (i + by) % peers) for i in range(peers)])


def nt_dot(left, right):
    return lax.dot_general(
        left, right, (((1,), (1,)), ((), ())), preferred_element_type=jnp.float32
    )


def self_product(amps):
    head = amps.astype(jnp.bfloat16)
    rest = (amps - head.astype(jnp.float32)).astype(jnp.bfloat16)
    return nt_dot(head, head) + nt_dot(head, rest) + nt_dot(rest, head)


def pair_amplitudes(pair, rows, cols, levels, virt_col, virt_rows, energy):
    row, col, slot = pair
    coupling = nt_dot(rows[row][...], cols[col][...])
    half = col % 2
    denominator = (
        virt_col[...]
        + virt_rows[half : half + 1, :]
        - levels[row]
        - levels[0 if col < 2 else 2]
    )
    amp = coupling / denominator
    lane = lax.broadcasted_iota(jnp.int32, energy.shape, 1)
    value = jnp.sum(amp * coupling, keepdims=True)
    return amp, energy + jnp.where(lane == slot, value, 0.0)


def add_pairs(pairs, rows, cols, levels, virt_col, virt_rows, density, energy):
    for pair in pairs:
        amp, energy = pair_amplitudes(pair, rows, cols, levels, virt_col, virt_rows, energy)
        density = density + self_product(amp)
    return density, energy


def own_kernel(levels, own, virt_col, virt_rows, density, energy):
    density[...], energy[...] = add_pairs(
        OWN_PAIRS,
        (own,),
        (own,),
        levels,
        virt_col,
        virt_rows,
        jnp.zeros(density.shape, jnp.float32),
        jnp.zeros(energy.shape, jnp.float32),
    )


def far_kernel(
    levels, own, own_mirror, far, virt_col, virt_rows, density_in, energy_in, density, energy
):
    density[...], energy[...] = add_pairs(
        FAR_PAIRS,
        (own,),
        (None, own_mirror, far),
        levels,
        virt_col,
        virt_rows,
        density_in[...],
        energy_in[...],
    )


def near_kernel(
    levels, own, own_mirror, near, far, virt_col, virt_rows, density_in, energy_in, density, energy
):
    density[...], energy[...] = add_pairs(
        NEAR_PAIRS,
        (None, near),
        (own, own_mirror, far),
        levels,
        virt_col,
        virt_rows,
        density_in[...],
        energy_in[...],
    )


def last_kernel(levels, own, near, far_mirror, virt_col, virt_rows, energy_in, amps, energy_out):
    energy = energy_in[...]
    for at, pair in enumerate(LAST_PAIRS):
        amps[at], energy = pair_amplitudes(
            pair,
            (own, near),
            (None, None, None, far_mirror),
            levels,
            virt_col,
            virt_rows,
            energy,
        )
    width = virt_col.shape[0]
    energy_out[...] = energy * (-1.0 / (width * width))


def spread_kernel(amps, density_in, spread, held):
    density = density_in[...]
    for at in range(amps.shape[0]):
        density = density + self_product(amps[at])
    width = density.shape[0]
    peers, each, stride = spread.shape
    panels = stride // LANES
    for panel in range(panels):
        part = density[:, panel * LANES : min(width, (panel + 1) * LANES)]
        if part.shape[1] < LANES:
            held[panel] = jnp.zeros(held.shape[1:], jnp.float32)
        held[panel, :, : part.shape[1]] = part
    for row in range(each):
        for panel in range(panels):
            spread[:, row, panel * LANES : (panel + 1) * LANES] = held[
                panel, pl.Slice(row, peers, each), :
            ]


def lookup_many(values_in, where_at):
    positions = jnp.arange(values_in.shape[0], dtype=jnp.int32)
    matches = positions[None, :] == where_at[:, None]
    return jnp.sum(
        jnp.where(matches, values_in[None, :], jnp.zeros_like(values_in)[None, :]), axis=1
    )


def call(kernel, out_shape, operands, smem, pairs, block, scratch=()):
    vmem = pl.BlockSpec(memory_space=pltpu.VMEM)
    specs = [pl.BlockSpec(memory_space=pltpu.SMEM)] * smem
    specs += [vmem] * (len(operands) - smem)
    width, depth = block.shape
    return pl.pallas_call(
        kernel,
        out_shape=out_shape,
        in_specs=specs,
        out_specs=jax.tree.map(lambda _: vmem, out_shape),
        scratch_shapes=list(scratch),
        compiler_params=pltpu.CompilerParams(vmem_limit_bytes=VMEM_BYTES),
        cost_estimate=pl.CostEstimate(
            flops=2 * pairs * width * width * depth,
            bytes_accessed=2 * pairs * width * depth,
            transcendentals=0,
        ),
    )(*operands)


def local(ints, occ_energy, occ_window, virt_energy):
    far = shifted(ints, "blk", 2)[0]
    near = shifted(ints, "blk", -1)[0]
    own_mirror = shifted(ints, "core", 1)[0]
    own = ints[0]
    width, depth = own.shape
    occ_count = occ_window.shape[0]
    peers = lax.axis_size("blk")
    group_index = lax.axis_index(GRP)
    block_index = lax.axis_index("blk")
    mirror_index = group_index + 1 - 2 * (group_index % 2)

    virt_own = lax.dynamic_slice_in_dim(virt_energy, group_index * width, width)
    virt_mirror = lax.dynamic_slice_in_dim(virt_energy, mirror_index * width, width)
    virt = (virt_own[:, None], jnp.stack([virt_own, virt_mirror]))
    wanted = (block_index + jnp.array([0, 1, -2], jnp.int32)) % peers
    levels = lookup_many(occ_energy, lookup_many(occ_window, wanted))

    sums = (
        jax.ShapeDtypeStruct((width, width), jnp.float32),
        jax.ShapeDtypeStruct((1, LANES), jnp.float32),
    )
    state = call(own_kernel, sums, (levels, own) + virt, 1, 1, own)
    far, density, energy = lax.optimization_barrier((far, *state))
    far_mirror = shifted(far, "core", 1)
    state = call(
        far_kernel, sums, (levels, own, own_mirror, far) + virt + (density, energy), 1, 2, own
    )
    state = call(
        near_kernel, sums, (levels, own, own_mirror, near, far) + virt + tuple(state), 1, 3, own
    )
    each = width // peers
    panels = -(-width // LANES)
    amps, energies = call(
        last_kernel,
        (jax.ShapeDtypeStruct((len(LAST_PAIRS), width, width), jnp.float32), sums[1]),
        (levels, own, near, far_mirror) + virt + (state[1],),
        1,
        2,
        own,
    )
    energies = energies[:, :STEPS]
    passed = shifted(energies, "blk", 1)
    spread = call(
        spread_kernel,
        jax.ShapeDtypeStruct((peers, each, panels * LANES), jnp.float32),
        (amps, state[0]),
        0,
        1,
        own,
        scratch=(pltpu.VMEM((panels, width, LANES), jnp.float32),),
    )
    odd = lax.broadcasted_iota(jnp.int32, energies.shape, 1) % 2 == 1
    passed, spread = lax.optimization_barrier((passed, spread))
    pair = lax.psum(jnp.where(odd, passed, energies), "core")
    pair, spread = lax.optimization_barrier((pair, spread))
    arrived = lax.all_to_all(spread, "blk", 0, 0, tiled=True)
    pair = lax.psum(pair, "z_hi")
    return arrived.sum(axis=0)[:, :width] * (1.0 / (occ_count * STEPS)), pair


def solution(mesh):
    peers = mesh.shape["blk"]
    finer = Mesh(mesh.devices.reshape(-1, 2, peers), ("z_hi", "core", "blk"))
    placed = (P("blk", GRP, None), P(), P(), P())
    return jax.shard_map(
        local,
        mesh=finer,
        in_specs=placed,
        out_specs=(P(GRP + ("blk",), None), P("blk", None)),
        check_vma=False,
    )
```

```python
import jax
import jax.numpy as jnp
from jax import lax
from jax.experimental import pallas as pl
from jax.experimental.pallas import tpu as pltpu
from jax.sharding import Mesh
from jax.sharding import PartitionSpec as P

STEPS = 4
LANES = 128
GRP = ("z_hi", "core")
VMEM_BYTES = 8 * 1024 * 1024
FAR_PAIRS = ((0, 2),)
NEAR_PAIRS = ((0, 1), (1, 0), (1, 1), (1, 2))
LAST_PAIRS = ((0, 3), (1, 3))


def shifted(shard, axis, by):
    peers = lax.axis_size(axis)
    return lax.ppermute(shard, axis, [(i, (i + by) % peers) for i in range(peers)])


def nt_dot(left, right):
    return lax.dot_general(
        left, right, (((1,), (1,)), ((), ())), preferred_element_type=jnp.float32
    )


def slot_of(row, col):
    return row + 2 * (col // 2)


def amplitude_of(row, col, rows, cols, inverse):
    coupling = nt_dot(rows[row][...], cols[col][...])
    amp = coupling * inverse[4 * row + col]
    return amp, amp * coupling


def add_energies(line, products):
    lane = lax.broadcasted_iota(jnp.int32, line.shape, 1)
    for slot in sorted({slot for slot, _ in products}):
        value = sum(array for at, array in products if at == slot)
        line = line + jnp.where(lane == slot, jnp.sum(value, keepdims=True), 0.0)
    return line


def add_squares(heads, cross, amps):
    for amp in amps:
        head = amp.astype(jnp.bfloat16)
        rest = (amp - head.astype(jnp.float32)).astype(jnp.bfloat16)
        heads = heads + nt_dot(head, head)
        cross = cross + nt_dot(head, rest)
    return heads, cross


def own_kernel(window, occ, virt, own, inverse, squares, energy):
    width = own.shape[0]
    orbitals = window.shape[0]
    group = 2 * lax.axis_index("z_hi") + lax.axis_index("core")
    block = lax.axis_index("blk")
    mirror = group + 1 - 2 * lax.rem(group, 2)
    row_own = jnp.zeros((1, width), jnp.float32)
    row_mirror = jnp.zeros((1, width), jnp.float32)
    for at in range(virt.shape[1] // width):
        row = virt[:, at * width : (at + 1) * width]
        row_own = jnp.where(group == at, row, row_own)
        row_mirror = jnp.where(mirror == at, row, row_mirror)
    down = lax.broadcasted_iota(jnp.int32, (width, width), 0)
    across = lax.broadcasted_iota(jnp.int32, (width, width), 1)
    col_own = jnp.sum(jnp.where(down == across, row_own, 0.0), axis=1, keepdims=True)
    level_own = occ[window[block]]
    level_next = occ[window[lax.rem(block + 1, orbitals)]]
    level_far = occ[window[lax.rem(block + orbitals - 2, orbitals)]]
    for row, level_row in enumerate((level_own, level_next)):
        for col in range(4):
            denominator = (
                col_own
                + (row_own if col % 2 == 0 else row_mirror)
                - level_row
                - (level_own if col < 2 else level_far)
            )
            inverse[4 * row + col] = 1.0 / denominator
    amp, product = amplitude_of(0, 0, (own,), (own,), inverse)
    energy[...] = add_energies(jnp.zeros(energy.shape, jnp.float32), [(0, product)])
    zero = jnp.zeros((width, width), jnp.float32)
    squares[0], squares[1] = add_squares(zero, zero, [amp])


def far_kernel(own, far, inverse, squares_in, energy_in, squares, energy):
    amps, products = [], []
    for row, col in FAR_PAIRS:
        amp, product = amplitude_of(row, col, (own,), (None, None, far), inverse)
        amps.append(amp)
        products.append((slot_of(row, col), product))
    energy[...] = add_energies(energy_in[...], products)
    squares[0], squares[1] = add_squares(squares_in[0], squares_in[1], amps)


def near_kernel(near, own, far, own_mirror, inverse, squares_in, energy_in, squares, energy):
    amps, products = [], []
    for row, col in NEAR_PAIRS:
        amp, product = amplitude_of(row, col, (own, near), (own, own_mirror, far), inverse)
        amps.append(amp)
        products.append((slot_of(row, col), product))
    energy[...] = add_energies(energy_in[...], products)
    squares[0], squares[1] = add_squares(squares_in[0], squares_in[1], amps)


def last_kernel(near, far_mirror, own, inverse, energy_in, amps, energy):
    products = []
    for at, (row, col) in enumerate(LAST_PAIRS):
        amp, product = amplitude_of(row, col, (own, near), (None, None, None, far_mirror), inverse)
        amps[at] = amp
        products.append((slot_of(row, col), product))
    width = own.shape[0]
    energy[...] = add_energies(energy_in[...], products) * (-1.0 / (width * width))


def spread_kernel(scale, amps, squares, spread, held):
    heads, cross = add_squares(
        squares[0], squares[1], [amps[at] for at in range(amps.shape[0])]
    )
    density = (heads + cross + cross.T) * scale
    width = density.shape[0]
    peers, each, stride = spread.shape
    panels = stride // LANES
    for panel in range(panels):
        part = density[:, panel * LANES : min(width, (panel + 1) * LANES)]
        if part.shape[1] < LANES:
            held[panel] = jnp.zeros(held.shape[1:], jnp.float32)
        held[panel, :, : part.shape[1]] = part
    for row in range(each):
        for panel in range(panels):
            spread[:, row, panel * LANES : (panel + 1) * LANES] = held[
                panel, pl.Slice(row, peers, each), :
            ]


def call(kernel, out_shape, operands, pairs, block, smem=0, scratch=()):
    vmem = pl.BlockSpec(memory_space=pltpu.VMEM)
    specs = [pl.BlockSpec(memory_space=pltpu.SMEM)] * smem
    specs += [vmem] * (len(operands) - smem)
    width, depth = block.shape
    return pl.pallas_call(
        kernel,
        out_shape=out_shape,
        in_specs=specs,
        out_specs=jax.tree.map(lambda _: vmem, out_shape),
        scratch_shapes=list(scratch),
        compiler_params=pltpu.CompilerParams(vmem_limit_bytes=VMEM_BYTES),
        cost_estimate=pl.CostEstimate(
            flops=2 * pairs * width * width * depth,
            bytes_accessed=2 * pairs * width * depth,
            transcendentals=0,
        ),
    )(*operands)


def local(ints, occ_energy, occ_window, virt_energy):
    far = shifted(ints, "blk", 2)[0]
    near = shifted(ints, "blk", -1)[0]
    own = ints[0]
    width = own.shape[0]
    occ_count = occ_window.shape[0]
    peers = lax.axis_size("blk")

    def squares_of(count):
        return jax.ShapeDtypeStruct((count, width, width), jnp.float32)

    line = jax.ShapeDtypeStruct((1, LANES), jnp.float32)
    inverse, squares, energy = call(
        own_kernel,
        (squares_of(8), squares_of(2), line),
        (occ_window, occ_energy, virt_energy[None, :], own),
        1,
        own,
        smem=2,
    )
    far, inverse, squares, energy = lax.optimization_barrier((far, inverse, squares, energy))
    far_mirror = shifted(far, "core", 1)
    own_mirror = shifted(ints, "core", 1)[0]
    squares, energy = call(
        far_kernel,
        (squares_of(2), line),
        (own, far, inverse, squares, energy),
        len(FAR_PAIRS),
        own,
    )
    squares, energy = call(
        near_kernel,
        (squares_of(2), line),
        (near, own, far, own_mirror, inverse, squares, energy),
        len(NEAR_PAIRS),
        own,
    )
    amps, energy = call(
        last_kernel,
        (squares_of(len(LAST_PAIRS)), line),
        (near, far_mirror, own, inverse, energy),
        len(LAST_PAIRS),
        own,
    )
    energy = energy[:, :STEPS]
    passed = shifted(energy, "blk", 1)
    each = width // peers
    panels = -(-width // LANES)
    scale = 1.0 / (occ_count * STEPS)
    spread = call(
        lambda *refs: spread_kernel(scale, *refs),
        jax.ShapeDtypeStruct((peers, each, panels * LANES), jnp.float32),
        (amps, squares),
        1,
        own,
        scratch=(pltpu.VMEM((panels, width, LANES), jnp.float32),),
    )
    odd = lax.broadcasted_iota(jnp.int32, energy.shape, 1) % 2 == 1
    passed, spread = lax.optimization_barrier((passed, spread))
    pair = lax.psum(jnp.where(odd, passed, energy), "core")
    pair, spread = lax.optimization_barrier((pair, spread))
    arrived = lax.all_to_all(spread, "blk", 0, 0, tiled=True)
    pair = lax.all_gather(pair, "z_hi", axis=0, tiled=True).sum(axis=0, keepdims=True)
    return arrived[:, :, :width].sum(axis=0), pair


def solution(mesh):
    peers = mesh.shape["blk"]
    finer = Mesh(mesh.devices.reshape(-1, 2, peers), ("z_hi", "core", "blk"))
    placed = (P("blk", GRP, None), P(), P(), P())
    return jax.shard_map(
        local,
        mesh=finer,
        in_specs=placed,
        out_specs=(P(GRP + ("blk",), None), P("blk", None)),
        check_vma=False,
    )
```

```python
import jax
import jax.numpy as jnp
from jax import lax
from jax.experimental import pallas as pl
from jax.experimental.pallas import tpu as pltpu
from jax.sharding import Mesh
from jax.sharding import PartitionSpec as P

STEPS = 4
LANES = 128
ROWS = 512
GRP = ("z_hi", "core")
VMEM_BYTES = 8 * 1024 * 1024
FAR_PAIRS = ((0, 2),)
NEAR_PAIRS = ((0, 1), (1, 0), (1, 1), (1, 2))
LAST_PAIRS = ((0, 3), (1, 3))


def shifted(shard, axis, by):
    peers = lax.axis_size(axis)
    return lax.ppermute(shard, axis, [(i, (i + by) % peers) for i in range(peers)])


def nt_dot(left, right):
    return lax.dot_general(
        left, right, (((1,), (1,)), ((), ())), preferred_element_type=jnp.float32
    )


def slot_of(row, col):
    return row + 2 * (col // 2)


def amplitude_of(row, col, rows, cols, inverse):
    coupling = nt_dot(rows[row][...], cols[col][...])
    amp = coupling * inverse[4 * row + col]
    return amp, amp * coupling


def add_energies(line, products):
    lane = lax.broadcasted_iota(jnp.int32, line.shape, 1)
    for slot in sorted({slot for slot, _ in products}):
        value = sum(array for at, array in products if at == slot)
        line = line + jnp.where(lane == slot, jnp.sum(value, keepdims=True), 0.0)
    return line


def add_squares(heads, cross, amps):
    for amp in amps:
        head = amp.astype(jnp.bfloat16)
        rest = (amp - head.astype(jnp.float32)).astype(jnp.bfloat16)
        heads = heads + nt_dot(head, head)
        cross = cross + nt_dot(head, rest)
    return heads, cross


def own_kernel(window, occ, virt, own, inverse, squares, energy):
    width = own.shape[0]
    orbitals = window.shape[0]
    group = 2 * lax.axis_index("z_hi") + lax.axis_index("core")
    block = lax.axis_index("blk")
    mirror = group + 1 - 2 * lax.rem(group, 2)
    row_own = jnp.zeros((1, width), jnp.float32)
    row_mirror = jnp.zeros((1, width), jnp.float32)
    for at in range(virt.shape[1] // width):
        row = virt[:, at * width : (at + 1) * width]
        row_own = jnp.where(group == at, row, row_own)
        row_mirror = jnp.where(mirror == at, row, row_mirror)
    down = lax.broadcasted_iota(jnp.int32, (width, width), 0)
    across = lax.broadcasted_iota(jnp.int32, (width, width), 1)
    col_own = jnp.sum(jnp.where(down == across, row_own, 0.0), axis=1, keepdims=True)
    level_own = occ[window[block]]
    level_next = occ[window[lax.rem(block + 1, orbitals)]]
    level_far = occ[window[lax.rem(block + orbitals - 2, orbitals)]]
    for row, level_row in enumerate((level_own, level_next)):
        for col in range(4):
            denominator = (
                col_own
                + (row_own if col % 2 == 0 else row_mirror)
                - level_row
                - (level_own if col < 2 else level_far)
            )
            inverse[4 * row + col] = 1.0 / denominator
    amp, product = amplitude_of(0, 0, (own,), (own,), inverse)
    energy[...] = add_energies(jnp.zeros(energy.shape, jnp.float32), [(0, product)])
    zero = jnp.zeros((width, width), jnp.float32)
    squares[0], squares[1] = add_squares(zero, zero, [amp])


def far_kernel(own, far, inverse, squares_in, energy_in, squares, energy):
    amps, products = [], []
    for row, col in FAR_PAIRS:
        amp, product = amplitude_of(row, col, (own,), (None, None, far), inverse)
        amps.append(amp)
        products.append((slot_of(row, col), product))
    energy[...] = add_energies(energy_in[...], products)
    squares[0], squares[1] = add_squares(squares_in[0], squares_in[1], amps)


def near_kernel(near, own, far, own_mirror, inverse, squares_in, energy_in, squares, energy):
    amps, products = [], []
    for row, col in NEAR_PAIRS:
        amp, product = amplitude_of(row, col, (own, near), (own, own_mirror, far), inverse)
        amps.append(amp)
        products.append((slot_of(row, col), product))
    energy[...] = add_energies(energy_in[...], products)
    squares[0], squares[1] = add_squares(squares_in[0], squares_in[1], amps)


def last_kernel(near, far_mirror, own, inverse, energy_in, amps, energy):
    products = []
    for at, (row, col) in enumerate(LAST_PAIRS):
        amp, product = amplitude_of(row, col, (own, near), (None, None, None, far_mirror), inverse)
        amps[at] = amp
        products.append((slot_of(row, col), product))
    width = own.shape[0]
    energy[...] = add_energies(energy_in[...], products) * (-1.0 / (width * width))


def spread_kernel(scale, amps, squares, spread, held):
    heads, cross = add_squares(
        squares[0], squares[1], [amps[at] for at in range(amps.shape[0])]
    )
    density = (heads + cross + cross.T) * scale
    width = density.shape[0]
    held[0] = density[:, :LANES]
    held[1, :, : width - LANES] = density[:, LANES:]
    peers = spread.shape[0]
    each = width // peers
    tails = []
    for row in range(each):
        spread[:, 0, row * LANES : (row + 1) * LANES] = held[0, pl.Slice(row, peers, each), :]
        tails.append(held[1, pl.Slice(row, peers, each), :][:, : width - LANES])
    tails.append(jnp.zeros_like(tails[0]))
    for at in range(0, each, 2):
        start = each * LANES + at * (width - LANES)
        spread[:, 0, start : start + LANES] = jnp.concatenate(tails[at : at + 2], axis=1)


def final_kernel(arrived, gathered, density, pair):
    total = jnp.sum(arrived[...], axis=0)
    each, width = density.shape
    rest = width - LANES
    for row in range(each):
        density[row : row + 1, :LANES] = total[:, row * LANES : (row + 1) * LANES]
        start = each * LANES + row * rest
        density[row : row + 1, LANES:] = total[:, start : start + rest]
    pair[...] = jnp.sum(gathered[...], axis=0, keepdims=True)


def call(kernel, out_shape, operands, pairs, block, smem=0, scratch=()):
    vmem = pl.BlockSpec(memory_space=pltpu.VMEM)
    specs = [pl.BlockSpec(memory_space=pltpu.SMEM)] * smem
    specs += [vmem] * (len(operands) - smem)
    width, depth = block.shape
    return pl.pallas_call(
        kernel,
        out_shape=out_shape,
        in_specs=specs,
        out_specs=jax.tree.map(lambda _: vmem, out_shape),
        scratch_shapes=list(scratch),
        compiler_params=pltpu.CompilerParams(vmem_limit_bytes=VMEM_BYTES),
        cost_estimate=pl.CostEstimate(
            flops=2 * pairs * width * width * depth,
            bytes_accessed=2 * pairs * width * depth,
            transcendentals=0,
        ),
    )(*operands)


def local(ints, occ_energy, occ_window, virt_energy):
    far = shifted(ints, "blk", 2)[0]
    near = shifted(ints, "blk", -1)[0]
    own = ints[0]
    width = own.shape[0]
    occ_count = occ_window.shape[0]
    peers = lax.axis_size("blk")

    def squares_of(count):
        return jax.ShapeDtypeStruct((count, width, width), jnp.float32)

    line = jax.ShapeDtypeStruct((1, LANES), jnp.float32)
    inverse, squares, energy = call(
        own_kernel,
        (squares_of(8), squares_of(2), line),
        (occ_window, occ_energy, virt_energy[None, :], own),
        1,
        own,
        smem=2,
    )
    far, inverse, squares, energy = lax.optimization_barrier((far, inverse, squares, energy))
    far_mirror = shifted(far, "core", 1)
    own_mirror = shifted(ints, "core", 1)[0]
    squares, energy = call(
        far_kernel,
        (squares_of(2), line),
        (own, far, inverse, squares, energy),
        len(FAR_PAIRS),
        own,
    )
    squares, energy = call(
        near_kernel,
        (squares_of(2), line),
        (near, own, far, own_mirror, inverse, squares, energy),
        len(NEAR_PAIRS),
        own,
    )
    amps, energy = call(
        last_kernel,
        (squares_of(len(LAST_PAIRS)), line),
        (near, far_mirror, own, inverse, energy),
        len(LAST_PAIRS),
        own,
    )
    energy = lax.psum(energy, "core")
    passed = shifted(jnp.broadcast_to(energy, (ROWS, LANES)), "blk", 1)[:1, :STEPS]
    energy, amps = lax.optimization_barrier((energy, amps))
    energy = energy[:, :STEPS]
    each = width // peers
    rest = width - LANES
    scale = 1.0 / (occ_count * STEPS)
    spread = call(
        lambda *refs: spread_kernel(scale, *refs),
        jax.ShapeDtypeStruct((peers, 1, each * LANES + (each + 1) * rest), jnp.float32),
        (amps, squares),
        1,
        own,
        scratch=(pltpu.VMEM((2, width, LANES), jnp.float32),),
    )
    odd = lax.broadcasted_iota(jnp.int32, energy.shape, 1) % 2 == 1
    pair = jnp.where(odd, passed, energy)
    arrived = lax.all_to_all(spread, "blk", 0, 0, tiled=True)
    gathered = lax.all_gather(pair, "z_hi", axis=0, tiled=True)
    shapes = (
        jax.ShapeDtypeStruct((each, width), jnp.float32),
        jax.ShapeDtypeStruct((1, STEPS), jnp.float32),
    )
    density, pair = call(final_kernel, shapes, (arrived, gathered), 0, own)
    return density, pair


def solution(mesh):
    peers = mesh.shape["blk"]
    finer = Mesh(mesh.devices.reshape(-1, 2, peers), ("z_hi", "core", "blk"))
    placed = (P("blk", GRP, None), P(), P(), P())
    return jax.shard_map(
        local,
        mesh=finer,
        in_specs=placed,
        out_specs=(P(GRP + ("blk",), None), P("blk", None)),
        check_vma=False,
    )
```

```python
import jax
import jax.numpy as jnp
from jax import lax
from jax.experimental import pallas as pl
from jax.experimental.pallas import tpu as pltpu
from jax.sharding import Mesh
from jax.sharding import PartitionSpec as P

STEPS = 4
LANES = 128
ROWS = 384
GRP = ("z_hi", "core")
VMEM_BYTES = 8 * 1024 * 1024
FAR_PAIRS = ((0, 2),)
NEAR_PAIRS = ((0, 1), (1, 0), (1, 1), (1, 2))
LAST_PAIRS = ((0, 3), (1, 3))


def shifted(shard, axis, by):
    peers = lax.axis_size(axis)
    return lax.ppermute(shard, axis, [(i, (i + by) % peers) for i in range(peers)])


def nt_dot(left, right):
    return lax.dot_general(
        left, right, (((1,), (1,)), ((), ())), preferred_element_type=jnp.float32
    )


def slot_of(row, col):
    return row + 2 * (col // 2)


def amplitude_of(row, col, rows, cols, inverse):
    coupling = nt_dot(rows[row][...], cols[col][...])
    amp = coupling * inverse[4 * row + col]
    return amp, amp * coupling


def add_energies(line, products):
    lane = lax.broadcasted_iota(jnp.int32, line.shape, 1)
    for slot in sorted({slot for slot, _ in products}):
        value = sum(array for at, array in products if at == slot)
        line = line + jnp.where(lane == slot, jnp.sum(value, keepdims=True), 0.0)
    return line


def add_squares(heads, cross, amps):
    for amp in amps:
        head = amp.astype(jnp.bfloat16)
        rest = (amp - head.astype(jnp.float32)).astype(jnp.bfloat16)
        heads = heads + nt_dot(head, head)
        cross = cross + nt_dot(head, rest)
    return heads, cross


def own_kernel(window, occ, virt, own, inverse, squares, energy):
    width = own.shape[0]
    orbitals = window.shape[0]
    group = 2 * lax.axis_index("z_hi") + lax.axis_index("core")
    block = lax.axis_index("blk")
    mirror = group + 1 - 2 * lax.rem(group, 2)
    row_own = jnp.zeros((1, width), jnp.float32)
    row_mirror = jnp.zeros((1, width), jnp.float32)
    for at in range(virt.shape[1] // width):
        row = virt[:, at * width : (at + 1) * width]
        row_own = jnp.where(group == at, row, row_own)
        row_mirror = jnp.where(mirror == at, row, row_mirror)
    down = lax.broadcasted_iota(jnp.int32, (width, width), 0)
    across = lax.broadcasted_iota(jnp.int32, (width, width), 1)
    col_own = jnp.sum(jnp.where(down == across, row_own, 0.0), axis=1, keepdims=True)
    level_own = occ[window[block]]
    level_next = occ[window[lax.rem(block + 1, orbitals)]]
    level_far = occ[window[lax.rem(block + orbitals - 2, orbitals)]]
    for row, level_row in enumerate((level_own, level_next)):
        for col in range(4):
            denominator = (
                col_own
                + (row_own if col % 2 == 0 else row_mirror)
                - level_row
                - (level_own if col < 2 else level_far)
            )
            inverse[4 * row + col] = 1.0 / denominator
    amp, product = amplitude_of(0, 0, (own,), (own,), inverse)
    energy[...] = add_energies(jnp.zeros(energy.shape, jnp.float32), [(0, product)])
    zero = jnp.zeros((width, width), jnp.float32)
    squares[0], squares[1] = add_squares(zero, zero, [amp])


def far_kernel(own, far, inverse, squares_in, energy_in, squares, energy):
    amps, products = [], []
    for row, col in FAR_PAIRS:
        amp, product = amplitude_of(row, col, (own,), (None, None, far), inverse)
        amps.append(amp)
        products.append((slot_of(row, col), product))
    energy[...] = add_energies(energy_in[...], products)
    squares[0], squares[1] = add_squares(squares_in[0], squares_in[1], amps)


def near_kernel(near, own, far, own_mirror, inverse, squares_in, energy_in, squares, energy):
    amps, products = [], []
    for row, col in NEAR_PAIRS:
        amp, product = amplitude_of(row, col, (own, near), (own, own_mirror, far), inverse)
        amps.append(amp)
        products.append((slot_of(row, col), product))
    energy[...] = add_energies(energy_in[...], products)
    squares[0], squares[1] = add_squares(squares_in[0], squares_in[1], amps)


def last_kernel(near, far_mirror, own, inverse, energy_in, amps, energy):
    products = []
    for at, (row, col) in enumerate(LAST_PAIRS):
        amp, product = amplitude_of(row, col, (own, near), (None, None, None, far_mirror), inverse)
        amps[at] = amp
        products.append((slot_of(row, col), product))
    width = own.shape[0]
    energy[...] = add_energies(energy_in[...], products) * (-1.0 / (width * width))


def spread_kernel(scale, amps, squares, spread, held):
    heads, cross = add_squares(
        squares[0], squares[1], [amps[at] for at in range(amps.shape[0])]
    )
    density = (heads + cross + cross.T) * scale
    width = density.shape[0]
    held[0] = density[:, :LANES]
    held[1, :, : width - LANES] = density[:, LANES:]
    peers = spread.shape[0]
    each = width // peers
    tails = []
    for row in range(each):
        spread[:, 0, row * LANES : (row + 1) * LANES] = held[0, pl.Slice(row, peers, each), :]
        tails.append(held[1, pl.Slice(row, peers, each), :][:, : width - LANES])
    tails.append(jnp.zeros_like(tails[0]))
    for at in range(0, each, 2):
        start = each * LANES + at * (width - LANES)
        spread[:, 0, start : start + LANES] = jnp.concatenate(tails[at : at + 2], axis=1)


def final_kernel(arrived, gathered, density, pair):
    total = jnp.sum(arrived[...], axis=0)
    each, width = density.shape
    rest = width - LANES
    for row in range(each):
        density[row : row + 1, :LANES] = total[:, row * LANES : (row + 1) * LANES]
        start = each * LANES + row * rest
        density[row : row + 1, LANES:] = total[:, start : start + rest]
    pair[...] = jnp.sum(gathered[...], axis=0, keepdims=True)


def call(kernel, out_shape, operands, pairs, block, smem=0, scratch=()):
    vmem = pl.BlockSpec(memory_space=pltpu.VMEM)
    specs = [pl.BlockSpec(memory_space=pltpu.SMEM)] * smem
    specs += [vmem] * (len(operands) - smem)
    width, depth = block.shape
    return pl.pallas_call(
        kernel,
        out_shape=out_shape,
        in_specs=specs,
        out_specs=jax.tree.map(lambda _: vmem, out_shape),
        scratch_shapes=list(scratch),
        compiler_params=pltpu.CompilerParams(vmem_limit_bytes=VMEM_BYTES),
        cost_estimate=pl.CostEstimate(
            flops=2 * pairs * width * width * depth,
            bytes_accessed=2 * pairs * width * depth,
            transcendentals=0,
        ),
    )(*operands)


def local(ints, occ_energy, occ_window, virt_energy):
    far = shifted(ints, "blk", 2)[0]
    near = shifted(ints, "blk", -1)[0]
    own = ints[0]
    width = own.shape[0]
    occ_count = occ_window.shape[0]
    peers = lax.axis_size("blk")

    def squares_of(count):
        return jax.ShapeDtypeStruct((count, width, width), jnp.float32)

    line = jax.ShapeDtypeStruct((1, LANES), jnp.float32)
    inverse, squares, energy = call(
        own_kernel,
        (squares_of(8), squares_of(2), line),
        (occ_window, occ_energy, virt_energy[None, :], own),
        1,
        own,
        smem=2,
    )
    far, inverse, squares, energy = lax.optimization_barrier((far, inverse, squares, energy))
    far_mirror = shifted(far, "core", 1)
    own_mirror = shifted(ints, "core", 1)[0]
    squares, energy = call(
        far_kernel,
        (squares_of(2), line),
        (own, far, inverse, squares, energy),
        len(FAR_PAIRS),
        own,
    )
    squares, energy = call(
        near_kernel,
        (squares_of(2), line),
        (near, own, far, own_mirror, inverse, squares, energy),
        len(NEAR_PAIRS),
        own,
    )
    amps, energy = call(
        last_kernel,
        (squares_of(len(LAST_PAIRS)), line),
        (near, far_mirror, own, inverse, energy),
        len(LAST_PAIRS),
        own,
    )
    swapped = shifted(energy, "core", 1)
    each = width // peers
    rest = width - LANES
    scale = 1.0 / (occ_count * STEPS)
    spread = call(
        lambda *refs: spread_kernel(scale, *refs),
        jax.ShapeDtypeStruct((peers, 1, each * LANES + (each + 1) * rest), jnp.float32),
        (amps, squares),
        1,
        own,
        scratch=(pltpu.VMEM((2, width, LANES), jnp.float32),),
    )
    swapped, spread = lax.optimization_barrier((swapped, spread))
    energy = energy + swapped
    passed = shifted(jnp.broadcast_to(energy, (ROWS, LANES)), "blk", 1)[:1, :STEPS]
    energy = energy[:, :STEPS]
    odd = lax.broadcasted_iota(jnp.int32, energy.shape, 1) % 2 == 1
    pair = jnp.where(odd, passed, energy)
    arrived = lax.all_to_all(spread, "blk", 0, 0, tiled=True)
    gathered = lax.all_gather(pair, "z_hi", axis=0, tiled=True)
    shapes = (
        jax.ShapeDtypeStruct((each, width), jnp.float32),
        jax.ShapeDtypeStruct((1, STEPS), jnp.float32),
    )
    density, pair = call(final_kernel, shapes, (arrived, gathered), 0, own)
    return density, pair


def solution(mesh):
    peers = mesh.shape["blk"]
    finer = Mesh(mesh.devices.reshape(-1, 2, peers), ("z_hi", "core", "blk"))
    placed = (P("blk", GRP, None), P(), P(), P())
    return jax.shard_map(
        local,
        mesh=finer,
        in_specs=placed,
        out_specs=(P(GRP + ("blk",), None), P("blk", None)),
        check_vma=False,
    )
```

```python
import jax
import jax.numpy as jnp
from jax import lax
from jax.experimental import pallas as pl
from jax.experimental.pallas import tpu as pltpu
from jax.sharding import Mesh
from jax.sharding import PartitionSpec as P

STEPS = 4
LANES = 128
ROWS = 384
GRP = ("z_hi", "core")
VMEM_BYTES = 8 * 1024 * 1024
FAR_PAIRS = ((0, 2),)
NEAR_PAIRS = ((0, 1), (1, 0), (1, 1), (1, 2))
LAST_PAIRS = ((0, 3), (1, 3))


def shifted(shard, axis, by):
    peers = lax.axis_size(axis)
    return lax.ppermute(shard, axis, [(i, (i + by) % peers) for i in range(peers)])


def nt_dot(left, right):
    return lax.dot_general(
        left, right, (((1,), (1,)), ((), ())), preferred_element_type=jnp.float32
    )


def slot_of(row, col):
    return 2 * row + col // 2


def amplitude_of(row, col, rows, cols, inverse):
    coupling = nt_dot(rows[row][...], cols[col][...])
    amp = coupling * inverse[4 * row + col]
    return amp, amp * coupling


def add_energies(line, products):
    lane = lax.broadcasted_iota(jnp.int32, line.shape, 1)
    for slot in sorted({slot for slot, _ in products}):
        value = sum(array for at, array in products if at == slot)
        line = line + jnp.where(lane == slot, jnp.sum(value, keepdims=True), 0.0)
    return line


def add_squares(heads, cross, amps):
    for amp in amps:
        head = amp.astype(jnp.bfloat16)
        rest = (amp - head.astype(jnp.float32)).astype(jnp.bfloat16)
        heads = heads + nt_dot(head, head)
        cross = cross + nt_dot(head, rest)
    return heads, cross


def own_kernel(window, occ, virt, own, inverse, squares, energy):
    width = own.shape[0]
    orbitals = window.shape[0]
    group = 2 * lax.axis_index("z_hi") + lax.axis_index("core")
    block = lax.axis_index("blk")
    mirror = group + 1 - 2 * lax.rem(group, 2)
    row_own = jnp.zeros((1, width), jnp.float32)
    row_mirror = jnp.zeros((1, width), jnp.float32)
    for at in range(virt.shape[1] // width):
        row = virt[:, at * width : (at + 1) * width]
        row_own = jnp.where(group == at, row, row_own)
        row_mirror = jnp.where(mirror == at, row, row_mirror)
    down = lax.broadcasted_iota(jnp.int32, (width, width), 0)
    across = lax.broadcasted_iota(jnp.int32, (width, width), 1)
    col_own = jnp.sum(jnp.where(down == across, row_own, 0.0), axis=1, keepdims=True)
    level_own = occ[window[block]]
    level_next = occ[window[lax.rem(block + 2, orbitals)]]
    level_far = occ[window[lax.rem(block + orbitals - 1, orbitals)]]
    for row, level_row in enumerate((level_own, level_next)):
        for col in range(4):
            denominator = (
                col_own
                + (row_own if col % 2 == 0 else row_mirror)
                - level_row
                - (level_own if col < 2 else level_far)
            )
            inverse[4 * row + col] = 1.0 / denominator
    amp, product = amplitude_of(0, 0, (own,), (own,), inverse)
    energy[...] = add_energies(jnp.zeros(energy.shape, jnp.float32), [(0, product)])
    zero = jnp.zeros((width, width), jnp.float32)
    squares[0], squares[1] = add_squares(zero, zero, [amp])


def far_kernel(own, far, inverse, squares_in, energy_in, squares, energy):
    amps, products = [], []
    for row, col in FAR_PAIRS:
        amp, product = amplitude_of(row, col, (own,), (None, None, far), inverse)
        amps.append(amp)
        products.append((slot_of(row, col), product))
    energy[...] = add_energies(energy_in[...], products)
    squares[0], squares[1] = add_squares(squares_in[0], squares_in[1], amps)


def near_kernel(near, own, far, own_mirror, inverse, squares_in, energy_in, squares, energy):
    amps, products = [], []
    for row, col in NEAR_PAIRS:
        amp, product = amplitude_of(row, col, (own, near), (own, own_mirror, far), inverse)
        amps.append(amp)
        products.append((slot_of(row, col), product))
    energy[...] = add_energies(energy_in[...], products)
    squares[0], squares[1] = add_squares(squares_in[0], squares_in[1], amps)


def last_kernel(near, far_mirror, own, inverse, energy_in, amps, energy):
    products = []
    for at, (row, col) in enumerate(LAST_PAIRS):
        amp, product = amplitude_of(row, col, (own, near), (None, None, None, far_mirror), inverse)
        amps[at] = amp
        products.append((slot_of(row, col), product))
    width = own.shape[0]
    energy[...] = add_energies(energy_in[...], products) * (-1.0 / (width * width))


def spread_kernel(scale, amps, squares, spread, held):
    heads, cross = add_squares(
        squares[0], squares[1], [amps[at] for at in range(amps.shape[0])]
    )
    density = (heads + cross + cross.T) * scale
    width = density.shape[0]
    held[0] = density[:, :LANES]
    held[1, :, : width - LANES] = density[:, LANES:]
    peers = spread.shape[0]
    each = width // peers
    tails = []
    for row in range(each):
        spread[:, 0, row * LANES : (row + 1) * LANES] = held[0, pl.Slice(row, peers, each), :]
        tails.append(held[1, pl.Slice(row, peers, each), :][:, : width - LANES])
    tails.append(jnp.zeros_like(tails[0]))
    for at in range(0, each, 2):
        start = each * LANES + at * (width - LANES)
        spread[:, 0, start : start + LANES] = jnp.concatenate(tails[at : at + 2], axis=1)


def final_kernel(arrived, gathered, density, pair):
    total = jnp.sum(arrived[...], axis=0)
    each, width = density.shape
    rest = width - LANES
    for row in range(each):
        density[row : row + 1, :LANES] = total[:, row * LANES : (row + 1) * LANES]
        start = each * LANES + row * rest
        density[row : row + 1, LANES:] = total[:, start : start + rest]
    pair[...] = jnp.sum(gathered[...], axis=0, keepdims=True)


def call(kernel, out_shape, operands, pairs, block, smem=0, scratch=()):
    vmem = pl.BlockSpec(memory_space=pltpu.VMEM)
    specs = [pl.BlockSpec(memory_space=pltpu.SMEM)] * smem
    specs += [vmem] * (len(operands) - smem)
    width, depth = block.shape
    return pl.pallas_call(
        kernel,
        out_shape=out_shape,
        in_specs=specs,
        out_specs=jax.tree.map(lambda _: vmem, out_shape),
        scratch_shapes=list(scratch),
        compiler_params=pltpu.CompilerParams(vmem_limit_bytes=VMEM_BYTES),
        cost_estimate=pl.CostEstimate(
            flops=2 * pairs * width * width * depth,
            bytes_accessed=2 * pairs * width * depth,
            transcendentals=0,
        ),
    )(*operands)


def local(ints, occ_energy, occ_window, virt_energy):
    far = shifted(ints, "blk", 1)[0]
    near = shifted(ints, "blk", -2)[0]
    own = ints[0]
    width = own.shape[0]
    occ_count = occ_window.shape[0]
    peers = lax.axis_size("blk")

    def squares_of(count):
        return jax.ShapeDtypeStruct((count, width, width), jnp.float32)

    line = jax.ShapeDtypeStruct((1, LANES), jnp.float32)
    inverse, squares, energy = call(
        own_kernel,
        (squares_of(8), squares_of(2), line),
        (occ_window, occ_energy, virt_energy[None, :], own),
        1,
        own,
        smem=2,
    )
    far, inverse, squares, energy = lax.optimization_barrier((far, inverse, squares, energy))
    far_mirror = shifted(far, "core", 1)
    own_mirror = shifted(ints, "core", 1)[0]
    squares, energy = call(
        far_kernel,
        (squares_of(2), line),
        (own, far, inverse, squares, energy),
        len(FAR_PAIRS),
        own,
    )
    squares, energy = call(
        near_kernel,
        (squares_of(2), line),
        (near, own, far, own_mirror, inverse, squares, energy),
        len(NEAR_PAIRS),
        own,
    )
    amps, energy = call(
        last_kernel,
        (squares_of(len(LAST_PAIRS)), line),
        (near, far_mirror, own, inverse, energy),
        len(LAST_PAIRS),
        own,
    )
    swapped = shifted(energy, "core", 1)
    each = width // peers
    rest = width - LANES
    scale = 1.0 / (occ_count * STEPS)
    spread = call(
        lambda *refs: spread_kernel(scale, *refs),
        jax.ShapeDtypeStruct((peers, 1, each * LANES + (each + 1) * rest), jnp.float32),
        (amps, squares),
        1,
        own,
        scratch=(pltpu.VMEM((2, width, LANES), jnp.float32),),
    )
    swapped, spread = lax.optimization_barrier((swapped, spread))
    energy = energy + swapped
    passed = shifted(jnp.broadcast_to(energy, (ROWS, LANES)), "blk", 2)[:1, :STEPS]
    energy = energy[:, :STEPS]
    later = lax.broadcasted_iota(jnp.int32, energy.shape, 1) >= 2
    pair = jnp.where(later, passed, energy)
    arrived = lax.all_to_all(spread, "blk", 0, 0, tiled=True)
    gathered = lax.all_gather(pair, "z_hi", axis=0, tiled=True)
    shapes = (
        jax.ShapeDtypeStruct((each, width), jnp.float32),
        jax.ShapeDtypeStruct((1, STEPS), jnp.float32),
    )
    density, pair = call(final_kernel, shapes, (arrived, gathered), 0, own)
    return density, pair


def solution(mesh):
    peers = mesh.shape["blk"]
    finer = Mesh(mesh.devices.reshape(-1, 2, peers), ("z_hi", "core", "blk"))
    placed = (P("blk", GRP, None), P(), P(), P())
    return jax.shard_map(
        local,
        mesh=finer,
        in_specs=placed,
        out_specs=(P(GRP + ("blk",), None), P("blk", None)),
        check_vma=False,
    )
```

```python
import jax
import jax.numpy as jnp
from jax import lax
from jax.experimental import pallas as pl
from jax.experimental.pallas import tpu as pltpu
from jax.sharding import Mesh
from jax.sharding import PartitionSpec as P

STEPS = 4
LANES = 128
ROWS = 384
GRP = ("z_hi", "core")
VMEM_BYTES = 8 * 1024 * 1024
FAR_PAIRS = ((0, 2),)
NEAR_PAIRS = ((0, 1), (1, 0), (1, 1), (1, 2))
LAST_PAIRS = ((0, 3), (1, 3))


def shifted(shard, axis, by):
    peers = lax.axis_size(axis)
    return lax.ppermute(shard, axis, [(i, (i + by) % peers) for i in range(peers)])


def nt_dot(left, right):
    return lax.dot_general(
        left, right, (((1,), (1,)), ((), ())), preferred_element_type=jnp.float32
    )


def slot_of(row, col):
    return row + 2 * (col // 2)


def amplitude_of(row, col, rows, cols, inverse):
    coupling = nt_dot(rows[row][...], cols[col][...])
    amp = coupling * inverse[4 * row + col]
    return amp, amp * coupling


def add_energies(line, products):
    lane = lax.broadcasted_iota(jnp.int32, line.shape, 1)
    for slot in sorted({slot for slot, _ in products}):
        value = sum(array for at, array in products if at == slot)
        line = line + jnp.where(lane == slot, jnp.sum(value, keepdims=True), 0.0)
    return line


def add_squares(heads, cross, amps):
    for amp in amps:
        head = amp.astype(jnp.bfloat16)
        rest = (amp - head.astype(jnp.float32)).astype(jnp.bfloat16)
        heads = heads + nt_dot(head, head)
        cross = cross + nt_dot(head, rest)
    return heads, cross


def own_kernel(window, occ, virt, own, inverse, squares, energy):
    width = own.shape[0]
    orbitals = window.shape[0]
    group = 2 * lax.axis_index("z_hi") + lax.axis_index("core")
    block = lax.axis_index("blk")
    mirror = group + 1 - 2 * lax.rem(group, 2)
    row_own = jnp.zeros((1, width), jnp.float32)
    row_mirror = jnp.zeros((1, width), jnp.float32)
    for at in range(virt.shape[1] // width):
        row = virt[:, at * width : (at + 1) * width]
        row_own = jnp.where(group == at, row, row_own)
        row_mirror = jnp.where(mirror == at, row, row_mirror)
    down = lax.broadcasted_iota(jnp.int32, (width, width), 0)
    across = lax.broadcasted_iota(jnp.int32, (width, width), 1)
    col_own = jnp.sum(jnp.where(down == across, row_own, 0.0), axis=1, keepdims=True)
    level_own = occ[window[block]]
    level_next = occ[window[lax.rem(block + 1, orbitals)]]
    level_far = occ[window[lax.rem(block + orbitals - 2, orbitals)]]
    for row, level_row in enumerate((level_own, level_next)):
        for col in range(4):
            denominator = (
                col_own
                + (row_own if col % 2 == 0 else row_mirror)
                - level_row
                - (level_own if col < 2 else level_far)
            )
            inverse[4 * row + col] = 1.0 / denominator
    amp, product = amplitude_of(0, 0, (own,), (own,), inverse)
    energy[...] = add_energies(jnp.zeros(energy.shape, jnp.float32), [(0, product)])
    zero = jnp.zeros((width, width), jnp.float32)
    squares[0], squares[1] = add_squares(zero, zero, [amp])


def far_kernel(own, far, inverse, squares_in, energy_in, squares, energy):
    amps, products = [], []
    for row, col in FAR_PAIRS:
        amp, product = amplitude_of(row, col, (own,), (None, None, far), inverse)
        amps.append(amp)
        products.append((slot_of(row, col), product))
    energy[...] = add_energies(energy_in[...], products)
    squares[0], squares[1] = add_squares(squares_in[0], squares_in[1], amps)


def near_kernel(near, own, far, own_mirror, inverse, squares_in, energy_in, density, energy):
    amps, products = [], []
    for row, col in NEAR_PAIRS:
        amp, product = amplitude_of(row, col, (own, near), (own, own_mirror, far), inverse)
        amps.append(amp)
        products.append((slot_of(row, col), product))
    energy[...] = add_energies(energy_in[...], products)
    heads, cross = add_squares(squares_in[0], squares_in[1], amps)
    density[...] = heads + cross + cross.T


def last_kernel(near, far_mirror, own, inverse, energy_in, amps, energy):
    products = []
    for at, (row, col) in enumerate(LAST_PAIRS):
        amp, product = amplitude_of(row, col, (own, near), (None, None, None, far_mirror), inverse)
        amps[at] = amp
        products.append((slot_of(row, col), product))
    width = own.shape[0]
    energy[...] = add_energies(energy_in[...], products) * (-1.0 / (width * width))


def spread_kernel(scale, amps, density_in, spread, held):
    density = density_in[...]
    for at in range(amps.shape[0]):
        head = amps[at].astype(jnp.bfloat16)
        rest = (amps[at] - head.astype(jnp.float32)).astype(jnp.bfloat16)
        density = density + nt_dot(head, head) + nt_dot(head, rest) + nt_dot(rest, head)
    density = density * scale
    width = density.shape[0]
    held[0] = density[:, :LANES]
    held[1, :, : width - LANES] = density[:, LANES:]
    peers = spread.shape[0]
    each = width // peers
    tails = []
    for row in range(each):
        spread[:, 0, row * LANES : (row + 1) * LANES] = held[0, pl.Slice(row, peers, each), :]
        tails.append(held[1, pl.Slice(row, peers, each), :][:, : width - LANES])
    tails.append(jnp.zeros_like(tails[0]))
    for at in range(0, each, 2):
        start = each * LANES + at * (width - LANES)
        spread[:, 0, start : start + LANES] = jnp.concatenate(tails[at : at + 2], axis=1)


def final_kernel(arrived, gathered, density, pair):
    total = jnp.sum(arrived[...], axis=0)
    each, width = density.shape
    rest = width - LANES
    for row in range(each):
        density[row : row + 1, :LANES] = total[:, row * LANES : (row + 1) * LANES]
        start = each * LANES + row * rest
        density[row : row + 1, LANES:] = total[:, start : start + rest]
    pair[...] = jnp.sum(gathered[...], axis=0, keepdims=True)


def call(kernel, out_shape, operands, pairs, block, smem=0, scratch=()):
    vmem = pl.BlockSpec(memory_space=pltpu.VMEM)
    specs = [pl.BlockSpec(memory_space=pltpu.SMEM)] * smem
    specs += [vmem] * (len(operands) - smem)
    width, depth = block.shape
    return pl.pallas_call(
        kernel,
        out_shape=out_shape,
        in_specs=specs,
        out_specs=jax.tree.map(lambda _: vmem, out_shape),
        scratch_shapes=list(scratch),
        compiler_params=pltpu.CompilerParams(vmem_limit_bytes=VMEM_BYTES),
        cost_estimate=pl.CostEstimate(
            flops=2 * pairs * width * width * depth,
            bytes_accessed=2 * pairs * width * depth,
            transcendentals=0,
        ),
    )(*operands)


def local(ints, occ_energy, occ_window, virt_energy):
    far = shifted(ints, "blk", 2)[0]
    near = shifted(ints, "blk", -1)[0]
    own = ints[0]
    width = own.shape[0]
    occ_count = occ_window.shape[0]
    peers = lax.axis_size("blk")

    def squares_of(count):
        return jax.ShapeDtypeStruct((count, width, width), jnp.float32)

    line = jax.ShapeDtypeStruct((1, LANES), jnp.float32)
    inverse, squares, energy = call(
        own_kernel,
        (squares_of(8), squares_of(2), line),
        (occ_window, occ_energy, virt_energy[None, :], own),
        1,
        own,
        smem=2,
    )
    far, inverse, squares, energy = lax.optimization_barrier((far, inverse, squares, energy))
    far_mirror = shifted(far, "core", 1)
    own_mirror = shifted(ints, "core", 1)[0]
    squares, energy = call(
        far_kernel,
        (squares_of(2), line),
        (own, far, inverse, squares, energy),
        len(FAR_PAIRS),
        own,
    )
    density, energy = call(
        near_kernel,
        (jax.ShapeDtypeStruct((width, width), jnp.float32), line),
        (near, own, far, own_mirror, inverse, squares, energy),
        len(NEAR_PAIRS),
        own,
    )
    amps, energy = call(
        last_kernel,
        (squares_of(len(LAST_PAIRS)), line),
        (near, far_mirror, own, inverse, energy),
        len(LAST_PAIRS),
        own,
    )
    swapped = shifted(energy, "core", 1)
    each = width // peers
    rest = width - LANES
    scale = 1.0 / (occ_count * STEPS)
    spread = call(
        lambda *refs: spread_kernel(scale, *refs),
        jax.ShapeDtypeStruct((peers, 1, each * LANES + (each + 1) * rest), jnp.float32),
        (amps, density),
        1,
        own,
        scratch=(pltpu.VMEM((2, width, LANES), jnp.float32),),
    )
    swapped, spread = lax.optimization_barrier((swapped, spread))
    energy = energy + swapped
    passed = shifted(jnp.broadcast_to(energy, (ROWS, LANES)), "blk", 1)[:1, :STEPS]
    energy = energy[:, :STEPS]
    odd = lax.broadcasted_iota(jnp.int32, energy.shape, 1) % 2 == 1
    pair = jnp.where(odd, passed, energy)
    arrived = lax.all_to_all(spread, "blk", 0, 0, tiled=True)
    gathered = lax.all_gather(pair, "z_hi", axis=0, tiled=True)
    shapes = (
        jax.ShapeDtypeStruct((each, width), jnp.float32),
        jax.ShapeDtypeStruct((1, STEPS), jnp.float32),
    )
    density, pair = call(final_kernel, shapes, (arrived, gathered), 0, own)
    return density, pair


def solution(mesh):
    peers = mesh.shape["blk"]
    finer = Mesh(mesh.devices.reshape(-1, 2, peers), ("z_hi", "core", "blk"))
    placed = (P("blk", GRP, None), P(), P(), P())
    return jax.shard_map(
        local,
        mesh=finer,
        in_specs=placed,
        out_specs=(P(GRP + ("blk",), None), P("blk", None)),
        check_vma=False,
    )
```
